256 devices in a mesh: section: 2 (over z_hi), dp: 8 (over x, core), tensor: 16 (over y, z_lo).
Axes of the slice: x: 4, y: 4, z: 8 (z_hi: 2, z_lo: 4; z = z_hi * 4 + z_lo), core: 2. Of those that a mesh axis runs over, the one named last changes fastest.
Arguments:
- hidden: bfloat16 [256, 16384], P('dp'), may hold values from -6 to 6
- query_weight: bfloat16 [2, 16384, 16384], P('section', 'dp', 'tensor'), may hold values from -0.046875 to 0.046875
- out_weight: bfloat16 [2, 16384, 16384], P('section', 'tensor', 'dp'), may hold values from -0.28125 to 0.28125
- key_cache: bfloat16 [2, 256, 256, 1024], P('section', 'dp', None, 'tensor'), may hold values from -400 to 400
- value_cache: bfloat16 [2, 256, 256, 1024], P('section', 'dp', None, 'tensor'), may hold values from -6 to 6
- cache_lengths: int32 [256], P('dp'), may hold values from 32 to 256, as said below
Outputs:
- layer_outputs: bfloat16 [2, 256, 16384], P('section', 'dp')
The draws below stay inside these ranges and needn't reach their ends.
Inputs may be any that keep to these rules, and one draw needn't show every extreme that they name: `cache_lengths`: in every aligned block of 32 rows some row has all 256 positions live.
All inputs are finite; a program needn't handle non-finite values.
Results may differ from the reference program's by a relative error of at most 0.01595.
Values may be sent and summed in bfloat16 or wider, within the bound.
No kernel may reach another device: no remote copies, remote signals or barrier semaphores. Data moves between devices by JAX's collectives and lax.ppermute only.
A program may use at most 64 MiB of HBM per device.

```python
import math
import jax
import jax.numpy as jnp
from jax import lax

D = 16384
HD = 128
HEADS_DEV = 8
LEN = 256
ROWS_DEV = 32
ROWS = 256
HEADS = 128
KVH = 8
HEAD_GROUPS = 16
LAYERS = 2


def draw_key_cache(key, part):
    key = jax.random.fold_in(key, 11)
    shape = (LAYERS, ROWS, LEN, KVH * HD)
    base = jax.random.normal(key, shape, jnp.float32)
    return base.astype(jnp.bfloat16)


def draw_cache_lengths(key, part):
    key = jax.random.fold_in(key, 5)
    first_key, second_key = jax.random.split(key)
    drawn = jax.random.randint(first_key, (ROWS,), LEN // 8, LEN + 1, jnp.int32)
    chosen = jax.random.randint(second_key, (ROWS // ROWS_DEV, 1), 0, ROWS_DEV, jnp.int32)
    full_rows = (jnp.arange(ROWS_DEV, dtype=jnp.int32)[None, :] == chosen).reshape(ROWS)
    return jnp.where(full_rows, LEN, drawn).astype(jnp.int32)


def with_spikes(values, rng, source, target, blocks, factor):
    owner, partner = [(jnp.arange(values.shape[dim]) // (values.shape[dim] // blocks)).reshape([-1 if axis == dim else 1 for axis in range(values.ndim)]) for dim in (source, target)]
    chosen = jax.random.permutation(rng, blocks)[partner]
    strong = (owner == chosen) | (owner == (partner + blocks // 2) % blocks)
    return jnp.where(strong, factor * values, values)


def block_scale(own_key, shape, shards, smallest, top_value):
    loudness, own = 1.0, jax.random.fold_in(own_key, 6)
    for dim, shards_of in shards:
        steps = jnp.exp(jax.random.uniform(jax.random.fold_in(own, dim), (shards_of,), jnp.float32, smallest / len(shards), top_value / len(shards)))
        loudness = loudness * jnp.repeat(steps, shape[dim] // shards_of).reshape([-1 if axis == dim else 1 for axis in range(len(shape))])
    return loudness


def noise(key, shape, spread, bound, cuts=(), kind=jnp.bfloat16):
    values = jax.random.normal(key, shape, jnp.float32) * spread
    if len(cuts) > 0:
        values = block_scale(key, shape, cuts, -0.22, 0.18) * values
    return jnp.clip(values, min=-bound, max=bound).astype(kind)


def noise_with(key, extent, scale, most, cuts, heavy, kind=jnp.bfloat16):
    result = scale * jax.random.normal(key, extent, jnp.float32)
    if cuts:
        result = result * block_scale(key, extent, cuts, -0.22, 0.18)
    return jnp.clip(with_spikes(result, jax.random.fold_in(key, 3), *heavy), -most, most).astype(kind)


def setup_inputs(seed: int = 0) -> dict:
    key_list = jax.random.split(jax.random.key(seed), 7)
    return {
        "hidden": noise(key_list[0], (ROWS, D), 1.0, 6.0, ((0, 8),)),
        "query_weight": noise(key_list[1], (LAYERS, D, HEADS * HD), D ** -0.5, 0.046875, ((0, 2), (1, 8), (2, 16))),
        "out_weight": noise_with(key_list[2], (LAYERS, HEADS * HD, D), (6.0 / (HEADS * HD) ** 0.5), 0.28125, ((0, 2), (1, 16), (2, 8)), (1, 2, 16, 2.0)),
        "key_cache": draw_key_cache(jax.random.fold_in(key_list[6], 71), 0),
        "value_cache": noise(key_list[4], (LAYERS, ROWS, LEN, KVH * HD), 1.0, 6.0, ((0, 2), (1, 8), (3, 16))),
        "cache_lengths": draw_cache_lengths(jax.random.fold_in(key_list[6], 71), 0),
    }


def reference(hidden, query_weight, out_weight, key_cache, value_cache, cache_lengths):
    group = HEADS // KVH
    state = hidden
    results = []
    live_mask = (jnp.arange(LEN, dtype=jnp.int32)[None, :] < cache_lengths[:, None])[:, None, None, :]
    for layer_index in range(LAYERS):
        wide_rows = state.astype(jnp.float32)
        normed = (wide_rows * lax.rsqrt(lax.optimization_barrier(jnp.mean(wide_rows * wide_rows, axis=-1, keepdims=True)) + 1e-05)).astype(jnp.bfloat16)
        queries = jnp.dot(normed, query_weight[layer_index], preferred_element_type=jnp.float32).astype(jnp.bfloat16)
        queries = queries.reshape(ROWS, KVH, group, HD)
        key_rows = key_cache[layer_index].reshape(ROWS, LEN, KVH, HD)
        value_rows = value_cache[layer_index].reshape(ROWS, LEN, KVH, HD)
        scores = jnp.einsum('rkgh,rlkh->rkgl', queries.astype(jnp.float32), key_rows.astype(jnp.float32)) / math.sqrt(HD)
        scores = jnp.where(live_mask, scores, -1e+30)
        row_max = lax.optimization_barrier(jnp.max(scores, axis=-1, keepdims=True))
        expd = jnp.where(live_mask, jnp.exp(scores - row_max), 0.0)
        weights_bf = (expd / lax.optimization_barrier(jnp.sum(expd, axis=-1, keepdims=True))).astype(jnp.bfloat16)
        attended = jnp.einsum('rkgl,rlkh->rkgh', weights_bf.astype(jnp.float32), value_rows.astype(jnp.float32)).astype(jnp.bfloat16)
        attended = attended.reshape(ROWS, HEAD_GROUPS, HEADS_DEV * HD)
        out_groups = out_weight[layer_index].reshape(HEAD_GROUPS, HEADS_DEV * HD, D)

        def add_group(total, pair):
            group_rows, group_weight = pair
            partial_value = jnp.dot(group_rows, group_weight, preferred_element_type=jnp.float32).astype(jnp.bfloat16)
            partial_value = lax.optimization_barrier(partial_value)
            return (total + partial_value.astype(jnp.float32), None)
        summed, _ = lax.scan(add_group, jnp.zeros((ROWS, D), jnp.float32), (jnp.swapaxes(attended, 0, 1), out_groups))
        summed_bf = lax.optimization_barrier(summed.astype(jnp.bfloat16))
        state = (wide_rows + summed_bf.astype(jnp.float32)).astype(jnp.bfloat16)
        results.append(state)
    return jnp.stack(results)
```

```python
import jax
import jax.numpy as jnp
from jax import lax
from jax.experimental import pallas as pl
from jax.experimental.pallas import tpu as pltpu
from jax.sharding import Mesh, PartitionSpec as P

DP = ("x", "c")
DEPTH = ("zh", "zl")
TENSOR = ("y", "zh", "zl")
PAIRED = ("x", "c", "zl")
BF = jnp.bfloat16
F32 = jnp.float32
VMEM = pl.BlockSpec(memory_space=pltpu.VMEM)
SMEM = pl.BlockSpec(memory_space=pltpu.SMEM)
LIMIT = 48 * 1024 * 1024


def call(kernel, out_shapes, in_specs, args, flops=0, name=None):
    single = not isinstance(out_shapes, (list, tuple))
    shapes = [out_shapes] if single else list(out_shapes)
    moved = sum(a.size * a.dtype.itemsize for a in list(args) + shapes)
    return pl.pallas_call(
        kernel,
        out_shape=out_shapes,
        in_specs=in_specs,
        out_specs=VMEM if single else [VMEM] * len(shapes),
        compiler_params=pltpu.CompilerParams(vmem_limit_bytes=LIMIT),
        cost_estimate=pl.CostEstimate(flops=flops, bytes_accessed=moved, transcendentals=0),
        name=name,
    )(*args)


def gathered(block, axes):
    count = lax.axis_size(axes)
    return [block] + [
        lax.ppermute(block, axes, [(i, (i + k) % count) for i in range(count)])
        for k in range(1, count)
    ]


def traded(blocks, axes):
    return lax.all_to_all(blocks, axes, split_axis=0, concat_axis=0, tiled=True)


def project(columns, weight_ref, out_ref):
    rows, depth = columns.shape
    width = weight_ref.shape[1]
    wide = columns[...].astype(F32)
    squares = jnp.sum(wide * wide, axis=1, keepdims=True)
    high = squares.astype(BF)
    rest = squares - high.astype(F32)
    middle = rest.astype(BF)
    low = (rest - middle.astype(F32)).astype(BF)
    lane = lax.broadcasted_iota(jnp.int32, (rows, 128), 1)
    out_ref[:, width:] = jnp.where(
        lane == 0,
        high.astype(F32),
        jnp.where(lane == 1, middle.astype(F32), jnp.where(lane == 2, low.astype(F32), 0.0)),
    ).astype(BF)

    @pl.loop(0, width // 256)
    def _(tile):
        span = pl.ds(pl.multiple_of(tile * 256, 256), 256)
        out_ref[:, span] = jnp.dot(
            columns[...], weight_ref[:, span], preferred_element_type=F32
        ).astype(BF)


def project_whole(columns_ref, weight_ref, out_ref):
    project(columns_ref, weight_ref, out_ref)


def project_chunks(place_ref, own_ref, one_ref, two_ref, three_ref, weight_ref, out_ref, held):
    y, z = place_ref[0], place_ref[1]
    for step, source in enumerate((own_ref, one_ref, two_ref, three_ref)):
        for depth in range(source.shape[0]):
            index = lax.rem(y - step + 4, 4) * 4 + lax.rem(z - depth + 4, 4)
            held[:, pl.ds(pl.multiple_of(index * 128, 128), 128)] = source[depth]
    project(held, weight_ref, out_ref)


def attend(place_ref, sums_ref, live_ref, key_ref, key_other_ref, value_ref, value_other_ref, out_ref):
    half = place_ref[2]
    rows = sums_ref.shape[1]
    width = sums_ref.shape[2] - 128
    sources = sums_ref.shape[0] // 2
    heads = []
    for part in range(2):
        total = sums_ref[part].astype(F32)
        for source in range(1, sources):
            total += sums_ref[2 * source + part].astype(F32)
        squares = total[:, width : width + 1] + total[:, width + 1 : width + 2]
        squares = squares + total[:, width + 2 : width + 3]
        scale = lax.rsqrt(squares / 16384.0 + 1e-05)
        scaled = total[:, :width] * scale
        heads += [scaled[:, h * 128 : (h + 1) * 128] for h in range(width // 128)]
    queries = jnp.concatenate(heads, axis=0)
    count = queries.shape[0]
    turned = pltpu.roll(queries, 64, 1)
    lane = lax.broadcasted_iota(jnp.int32, (count, 128), 1)
    row = lax.rem(lax.broadcasted_iota(jnp.int32, (count, 128), 0), rows)
    first = lane < 64
    low = jnp.where(first, queries, turned)
    high = jnp.where(first, turned, queries)
    is_low = half == 0
    own_q = jnp.where(is_low, low, high)
    other_q = jnp.where(is_low, high, low)

    def spread(block):
        return jnp.concatenate(
            [
                jnp.where(row == 2 * k + jnp.where(first, 0, 1), block, 0.0).astype(BF)
                for k in range(rows // 2)
            ],
            axis=1,
        )

    mine = pl.ds(half * rows, rows)
    depth = key_ref.shape[1]
    cache_len = key_ref.shape[2]
    own_key = key_ref[mine].reshape(rows * depth, cache_len)
    other_key = key_other_ref[...].reshape(rows * depth, cache_len)
    scores = jnp.dot(spread(own_q), own_key, preferred_element_type=F32)
    scores += jnp.dot(spread(other_q), other_key, preferred_element_type=F32)
    scores = scores * (128.0**-0.5)
    position = lax.broadcasted_iota(jnp.int32, scores.shape, 1)
    live = position < live_ref[...]
    scores = jnp.where(live, scores, -1e30)
    top = jnp.max(scores, axis=1, keepdims=True)
    expd = jnp.where(live, jnp.exp(scores - top), 0.0)
    probs = (expd / jnp.sum(expd, axis=1, keepdims=True)).astype(BF)

    def blend(values):
        flat = values.reshape(rows * depth, cache_len)
        product = lax.dot_general(
            probs, flat, (((1,), (1,)), ((), ())), preferred_element_type=F32
        )
        total = jnp.zeros((count, 128), F32)
        for k in range(rows // 2):
            total += jnp.where(row // 2 == k, product[:, k * 128 : (k + 1) * 128], 0.0)
        return total

    own = blend(value_ref[mine])
    other = blend(value_other_ref[...])
    odd = lax.rem(row, 2)
    own = jnp.where(odd == half, own, pltpu.roll(own, 64, 1))
    other = jnp.where(odd == half, pltpu.roll(other, 64, 1), other)
    attended = jnp.where(jnp.where(first, 0, 1) == half, own, other).astype(BF)
    for part in range(2):
        for h in range(width // 128):
            start = (part * (width // 128) + h) * rows
            tile = attended[start : start + rows]
            for target in range(sources):
                out_ref[2 * target + part, :, h * 128 : (h + 1) * 128] = tile


def emit(rows_ref, weight_ref, out_ref):
    tiles = out_ref.shape[0] // 2

    @pl.loop(0, tiles)
    def _(tile):
        span = pl.ds(pl.multiple_of(tile * 256, 256), 256)
        product = jnp.dot(rows_ref[...], weight_ref[:, span], preferred_element_type=F32).astype(BF)
        out_ref[2 * tile] = product[:, :128]
        out_ref[2 * tile + 1] = product[:, 128:]


def merge(blocks_ref, out_ref):
    total = blocks_ref[0].astype(F32)
    for source in range(1, blocks_ref.shape[0]):
        total += blocks_ref[source].astype(F32)
    out_ref[...] = total.astype(BF)


def merge_state(blocks_ref, state_ref, out_ref):
    total = blocks_ref[0].astype(F32)
    for source in range(1, blocks_ref.shape[0]):
        total += blocks_ref[source].astype(F32)
    total = total.astype(BF).astype(F32)
    out_ref[...] = (state_ref[...].astype(F32) + total).astype(BF)


def lay_out(place_ref, own_ref, one_ref, two_ref, three_ref, out_ref):
    y, z = place_ref[0], place_ref[1]
    for step, source in enumerate((own_ref, one_ref, two_ref, three_ref)):
        for depth in range(4):
            index = lax.rem(y - step + 4, 4) * 4 + lax.rem(z - depth + 4, 4)
            for part in range(8):
                start = pl.multiple_of(index * 128 + part * 2048, 128)
                out_ref[:, pl.ds(start, 128)] = source[depth, part]


def layer(partial, state, place, live, out_weight, key, key_other, value, value_other):
    rows, wide = partial.shape
    sums = traded(partial.reshape(16, rows // 16, wide), PAIRED)
    sent = call(
        attend,
        jax.ShapeDtypeStruct((16, rows // 16, wide - 128), BF),
        [SMEM] + [VMEM] * 6,
        (place, sums, live, key, key_other, value, value_other),
        flops=4 * rows * 2048 * 256,
        name="attend",
    )
    attended = traded(sent, PAIRED).reshape(rows, wide - 128)
    blocks = call(
        emit,
        jax.ShapeDtypeStruct((16, rows, 128), BF),
        [VMEM, VMEM],
        (attended, out_weight),
        flops=2 * rows * 1024 * 2048,
        name="emit",
    )
    blocks = traded(blocks.reshape(4, 4, rows, 128), "y")
    blocks = call(merge, jax.ShapeDtypeStruct((4, rows, 128), BF), [VMEM], (blocks,), name="merge")
    blocks = traded(blocks, DEPTH)
    return call(
        merge_state,
        jax.ShapeDtypeStruct((rows, 128), BF),
        [VMEM, VMEM],
        (blocks, state),
        name="merge_state",
    )


def body(hidden, query_weight, out_weight, key_cache, value_cache, cache_lengths):
    y = lax.axis_index("y")
    z = lax.axis_index(DEPTH)
    half = lax.axis_index("zl")
    place = jnp.stack([y, z, half]).astype(jnp.int32)
    query_weight, out_weight = query_weight[0], out_weight[0]
    key = jnp.swapaxes(key_cache[0], 1, 2)
    value = jnp.swapaxes(value_cache[0], 1, 2)
    swap = [(0, 1), (1, 0)]
    far = (1 - half) * 16
    key_other = lax.ppermute(lax.dynamic_slice_in_dim(key, far, 16, 0), "zl", swap)
    value_other = lax.ppermute(lax.dynamic_slice_in_dim(value, far, 16, 0), "zl", swap)
    lengths = lax.dynamic_slice_in_dim(cache_lengths, half * 16, 16, 0)
    live = jnp.tile(lengths, 16)[:, None]

    rows_here, wide = hidden.shape
    columns = traded(jnp.swapaxes(hidden.reshape(rows_here, 8, wide // 8), 0, 1), DP)
    columns = columns.reshape(8 * rows_here, wide // 8)
    rows = columns.shape[0]
    state = lax.dynamic_slice_in_dim(columns, (y * 4 + z) * 128, 128, 1)
    partial_shape = jax.ShapeDtypeStruct((rows, query_weight.shape[1] + 128), BF)
    flops = 2 * rows * query_weight.shape[0] * query_weight.shape[1]
    partial = call(
        project_whole, partial_shape, [VMEM, VMEM], (columns, query_weight), flops, "project"
    )
    caches = (out_weight, key, key_other, value, value_other)
    first = layer(partial, state, place, live, *caches)

    arrived = lax.ppermute(first, "s", [(0, 1)])
    chunks = gathered(jnp.stack(gathered(arrived, DEPTH)), "y")
    partial = pl.pallas_call(
        project_chunks,
        out_shape=partial_shape,
        in_specs=[SMEM] + [VMEM] * 5,
        out_specs=VMEM,
        scratch_shapes=[pltpu.VMEM((rows, wide // 8), BF)],
        compiler_params=pltpu.CompilerParams(vmem_limit_bytes=LIMIT),
        cost_estimate=pl.CostEstimate(flops=flops, bytes_accessed=6 << 20, transcendentals=0),
        name="project_chunks",
    )(place, *chunks, query_weight)
    second = layer(partial, arrived, place, live, *caches)

    result = jnp.where(lax.axis_index("s") == 0, first, second)
    result = traded(result.reshape(8, rows_here, 128), DP)
    pieces = gathered(jnp.stack(gathered(result, DEPTH)), "y")
    out = call(
        lay_out,
        jax.ShapeDtypeStruct((rows_here, wide), BF),
        [SMEM] + [VMEM] * 4,
        (place, *pieces),
        name="lay_out",
    )
    return out[None]


def solution(mesh):
    fine = Mesh(mesh.devices.reshape(2, 4, 2, 4, 2, 2), ("s", "x", "c", "y", "zh", "zl"))
    in_specs = (
        P(DP, None),
        P("s", DP, TENSOR),
        P("s", TENSOR, DP),
        P("s", DP, None, TENSOR),
        P("s", DP, None, TENSOR),
        P(DP),
    )
    out_specs = P("s", DP, None)
    return jax.shard_map(body, mesh=fine, in_specs=in_specs, out_specs=out_specs, check_vma=False)
```

```python
import functools

import jax
import jax.numpy as jnp
from jax import lax
from jax.experimental import pallas as pl
from jax.experimental.pallas import tpu as pltpu
from jax.sharding import Mesh, PartitionSpec as P

DP = ("x", "c")
DEPTH = ("zh", "zl")
TENSOR = ("y", "zh", "zl")
BF = jnp.bfloat16
F32 = jnp.float32
VMEM = pl.BlockSpec(memory_space=pltpu.VMEM)
HBM = pl.BlockSpec(memory_space=pltpu.HBM)
SMEM = pl.BlockSpec(memory_space=pltpu.SMEM)
LIMIT = 16 * 1024 * 1024
GROUP = 16
Y, Z, HALF, SECTION, X, CORE = range(6)


def call(kernel, out_shapes, args, flops=0, scratch=(), remote=(), name=None):
    single = not isinstance(out_shapes, (list, tuple))
    shapes = [out_shapes] if single else list(out_shapes)
    volume = sum(a.size * a.dtype.itemsize for a in list(args) + shapes)
    return pl.pallas_call(
        kernel,
        out_shape=out_shapes,
        in_specs=[
            HBM if k in remote else SMEM if a.ndim == 1 else VMEM for k, a in enumerate(args)
        ],
        out_specs=VMEM if single else [VMEM] * len(shapes),
        scratch_shapes=list(scratch),
        compiler_params=pltpu.CompilerParams(vmem_limit_bytes=LIMIT),
        cost_estimate=pl.CostEstimate(flops=flops, bytes_accessed=volume, transcendentals=0),
        name=name,
    )(*args)


def moved(block, axes, step):
    count = lax.axis_size(axes)
    if step % count == 0:
        return block
    return lax.ppermute(block, axes, [(i, (i + step) % count) for i in range(count)])


def gathered(block, axes):
    return [moved(block, axes, step) for step in range(lax.axis_size(axes))]


def arrange(place_ref, hidden_ref, *refs):
    out_refs, done = refs[:8], refs[8]
    x, core = place_ref[X], place_ref[CORE]
    width = out_refs[0].shape[1]
    copies = []
    for index, out_ref in enumerate(out_refs):
        side, step = 1 - index // 4, index % 4
        part = lax.rem(x + step, 4) * 2 + lax.rem(core + side, 2)
        columns = hidden_ref.at[:, pl.ds(pl.multiple_of(part * width, 128), width)]
        copies.append(pltpu.make_async_copy(columns, out_ref, done.at[index]))
        copies[-1].start()
    for copy in copies:
        copy.wait()


def pick(*refs):
    out_ref = refs[-1]
    for step, ref in enumerate(refs[:-1]):
        out_ref[step] = ref[...]


def project(held, weight_ref, near_ref, far_ref):
    rows = near_ref.shape[0]
    width = weight_ref.shape[1]
    for start, out_ref in ((rows, far_ref), (0, near_ref)):
        wide = held[start : start + rows].astype(F32)
        squares = jnp.sum(wide * wide, axis=1, keepdims=True)
        high = squares.astype(BF).astype(F32)
        middle = (squares - high).astype(BF).astype(F32)
        low = squares - high - middle
        lane = lax.broadcasted_iota(jnp.int32, (rows, 128), 1)
        pieces = jnp.where(lane == 0, high, jnp.where(lane == 1, middle, low))
        out_ref[:, width:] = jnp.where(lane < 3, pieces, 0.0).astype(BF)

    for tile in range(width // 256):
        span = slice(tile * 256, (tile + 1) * 256)
        product = jnp.dot(held[...], weight_ref[:, span], preferred_element_type=F32).astype(BF)
        near_ref[:, span] = product[:rows]
        far_ref[:, span] = product[rows:]


def project_rows(place_ref, a_ref, b_ref, c_ref, d_ref, other_ref, weight_ref, *refs):
    near_ref, far_ref, state_ref, held = refs
    rows = a_ref.shape[0]
    for step, ref in enumerate((a_ref, b_ref, c_ref, d_ref)):
        held[step * rows : (step + 1) * rows] = ref[...]
        held[(step + 4) * rows : (step + 5) * rows] = other_ref[step]
    start = (place_ref[Y] * 4 + place_ref[Z]) * 128
    state_ref[...] = held[:, pl.ds(pl.multiple_of(start, 128), 128)]
    project(held, weight_ref, near_ref, far_ref)


def project_columns(place_ref, *refs):
    pieces, weight_ref, near_ref, far_ref, held = refs[:8], refs[8], refs[9], refs[10], refs[11]
    y, z = place_ref[Y], place_ref[Z]
    for step in range(4):
        for depth in range(4):
            index = lax.rem(y - step + 4, 4) * 4 + 3 - lax.rem(z - depth + 4, 4)
            piece = pieces[step][...] if depth == 0 else pieces[4 + step][depth - 1]
            held[:, pl.ds(pl.multiple_of(index * 128, 128), 128)] = piece
    project(held, weight_ref, near_ref, far_ref)


def add_cores(near_ref, far_ref, *out_refs):
    rows = out_refs[0].shape[0]
    for step, out_ref in enumerate(out_refs):
        span = slice(step * rows, (step + 1) * rows)
        out_ref[...] = (near_ref[span].astype(F32) + far_ref[span].astype(F32)).astype(BF)


def queries_of(sums, width):
    total = sums[0][...].astype(F32)
    for block in sums[1:]:
        total += block[...].astype(F32)
    squares = total[:, width : width + 1] + total[:, width + 1 : width + 2]
    squares = squares + total[:, width + 2 : width + 3]
    return total[:, :width] * lax.rsqrt(squares / 16384.0 + 1e-05)


def group_attention(half, queries, heads, lengths_ref, start, caches):
    key, key_other, value, value_other = caches
    depth, cache_len = key.shape[1:]
    count = GROUP * heads
    lane = lax.broadcasted_iota(jnp.int32, (count, 128), 1)
    row = lax.rem(lax.broadcasted_iota(jnp.int32, (count, 128), 0), GROUP)
    first = lane < 64
    side = jnp.where(first, 0, 1)
    odd = lax.rem(row, 2)

    def diagonal(block):
        return jnp.concatenate(
            [jnp.where(row == 2 * k + side, block, 0.0).astype(BF) for k in range(GROUP // 2)],
            axis=1,
        )

    def blend(values):
        product = lax.dot_general(
            probs,
            values.reshape(GROUP * depth, cache_len),
            (((1,), (1,)), ((), ())),
            preferred_element_type=F32,
        )
        result = jnp.zeros((count, 128), F32)
        for k in range(GROUP // 2):
            result += jnp.where(row // 2 == k, product[:, k * 128 : (k + 1) * 128], 0.0)
        return result

    turned = pltpu.roll(queries, 64, 1)
    low = jnp.where(first, queries, turned)
    high = jnp.where(first, turned, queries)
    own_q = jnp.where(half == 0, low, high)
    other_q = jnp.where(half == 0, high, low)
    key = key.reshape(GROUP * depth, cache_len)
    key_other = key_other.reshape(GROUP * depth, cache_len)
    scores = jnp.dot(diagonal(own_q), key, preferred_element_type=F32)
    scores += jnp.dot(diagonal(other_q), key_other, preferred_element_type=F32)
    scores = scores * (128.0**-0.5)
    limits = jnp.zeros((count, 128), jnp.int32)
    for k in range(GROUP):
        limits = jnp.where(row == k, lengths_ref[start + k], limits)
    limits = jnp.concatenate([limits] * (cache_len // 128), axis=1)
    live = lax.broadcasted_iota(jnp.int32, scores.shape, 1) < limits
    scores = jnp.where(live, scores, -1e30)
    top = jnp.max(scores, axis=1, keepdims=True)
    expd = jnp.where(live, jnp.exp(scores - top), 0.0)
    probs = (expd / jnp.sum(expd, axis=1, keepdims=True)).astype(BF)
    own = blend(value)
    other = blend(value_other)
    own = jnp.where(odd == half, own, pltpu.roll(own, 64, 1))
    other = jnp.where(odd == half, pltpu.roll(other, 64, 1), other)
    return jnp.where(side == half, own, other).astype(BF)


def stacked(block, heads):
    return jnp.concatenate([block[:, h * 128 : (h + 1) * 128] for h in range(heads)], axis=0)


def share_rows(place_ref, a_ref, b_ref, c_ref, d_ref, mine_ref, theirs_ref):
    half = place_ref[HALF]
    queries = queries_of((a_ref, b_ref, c_ref, d_ref), mine_ref.shape[1])
    top, bottom = queries[:GROUP], queries[GROUP:]
    mine_ref[...] = jnp.where(half == 0, top, bottom).astype(BF)
    theirs_ref[...] = jnp.where(half == 0, bottom, top).astype(BF)


def attend_pair(place_ref, lengths_ref, mine_ref, partner_ref, *refs):
    key_ref, value_ref, other_ref, own_ref, theirs_ref = refs
    half = place_ref[HALF]
    heads = mine_ref.shape[1] // 128
    blocks = [stacked(ref[...].astype(F32), heads) for ref in (mine_ref, partner_ref)]
    span = pl.ds(half * GROUP, GROUP)
    caches = (key_ref[span], other_ref[0], value_ref[span], other_ref[1])
    attended = group_attention(
        half, jnp.concatenate(blocks, axis=0), 2 * heads, lengths_ref, half * GROUP, caches
    )
    for index, out_ref in enumerate((own_ref, theirs_ref)):
        for h in range(heads):
            start = (index * heads + h) * GROUP
            out_ref[:, h * 128 : (h + 1) * 128] = attended[start : start + GROUP]


def rejoin(place_ref, own_ref, received_ref, out_ref):
    half = place_ref[HALF]
    out_ref[:GROUP] = jnp.where(half == 0, own_ref[...], received_ref[...])
    out_ref[GROUP:] = jnp.where(half == 0, received_ref[...], own_ref[...])


def attend(place_ref, lengths_ref, a_ref, b_ref, c_ref, d_ref, *refs):
    key_ref, value_ref, near_ref, far_ref, out_ref = refs
    half = place_ref[HALF]
    heads = out_ref.shape[1] // 128
    queries = queries_of((a_ref, b_ref, c_ref, d_ref), out_ref.shape[1])
    for near in (True, False):
        index = half if near else 1 - half
        start = pl.multiple_of(index * GROUP, GROUP)
        mine = jnp.where(index == 0, queries[:GROUP], queries[GROUP:])
        caches = (
            key_ref[pl.ds(start, GROUP)],
            (near_ref if near else far_ref)[0],
            value_ref[pl.ds(start, GROUP)],
            (near_ref if near else far_ref)[1],
        )
        attended = group_attention(half, stacked(mine, heads), heads, lengths_ref, start, caches)
        for h in range(heads):
            out_ref[pl.ds(start, GROUP), h * 128 : (h + 1) * 128] = attended[
                h * GROUP : (h + 1) * GROUP
            ]


def take_half(index_ref, key_ref, value_ref, out_ref, done):
    span = pl.ds(index_ref[0] * GROUP, GROUP)
    copies = [
        pltpu.make_async_copy(ref.at[span], out_ref.at[k], done.at[k])
        for k, ref in enumerate((key_ref, value_ref))
    ]
    for copy in copies:
        copy.start()
    for copy in copies:
        copy.wait()


def row_half(index, key, value):
    return call(
        take_half,
        jax.ShapeDtypeStruct((2, GROUP, *key.shape[1:]), BF),
        (index, key, value),
        scratch=[pltpu.SemaphoreType.DMA((2,))],
        remote=(1, 2),
        name="take_half",
    )


def emit(mirrored, place_ref, *refs):
    blocks, weight_ref, out_refs, held = refs[:8], refs[8], refs[9:17], refs[17]
    y, z = place_ref[Y], place_ref[Z]
    rows = blocks[0].shape[0]
    for index, block in enumerate(blocks):
        held[index * rows : (index + 1) * rows] = block[...]
    for half, depths in enumerate(((1, 2), (3, 0))):
        for step in range(4):
            columns = []
            for depth in depths:
                column = lax.rem(z + depth, 4)
                column = 3 - column if mirrored else column
                start = pl.multiple_of((lax.rem(y + step, 4) * 4 + column) * 128, 128)
                columns.append(weight_ref[:, pl.ds(start, 128)])
            product = jnp.dot(
                held[...], jnp.concatenate(columns, axis=1), preferred_element_type=F32
            ).astype(BF)
            out_refs[4 * half + step][0] = product[:, :128]
            out_refs[4 * half + step][1] = product[:, 128:]


def merge(*refs):
    sources, targets = refs[:4], refs[4:]
    for index, target in enumerate(targets):
        total = sources[0][index].astype(F32)
        for source in sources[1:]:
            total += source[index].astype(F32)
        target[...] = total.astype(BF)


def updated(sources, state):
    total = sources[0][...].astype(F32)
    for source in sources[1:]:
        total += source[...].astype(F32)
    total = total.astype(BF).astype(F32)
    return (state.astype(F32) + total).astype(BF)


def merge_state(*refs):
    sources, state_ref, out_ref = refs[:4], refs[4], refs[5]
    out_ref[...] = updated(sources, state_ref[...])


def merge_last(place_ref, *refs):
    sources, state_ref, first_ref, out_ref = refs[:4], refs[4], refs[5], refs[6]
    result = updated(sources, state_ref[...]).astype(F32)
    result = jnp.where(place_ref[SECTION] == 0, first_ref[...].astype(F32), result).astype(BF)
    rows = out_ref.shape[1]
    for side in range(2):
        for step in range(4):
            owner = lax.rem(place_ref[X] - step + 4, 4) * 2 + lax.rem(place_ref[CORE] + side, 2)
            start = (side * 4 + step) * rows
            out_ref[owner] = result[start : start + rows]


def lay_out(place_ref, *refs):
    y, z = place_ref[Y], place_ref[Z]
    out_ref = refs[-1]
    for step in range(4):
        for depth in range(4):
            column = lax.rem(z - depth + 4, 4)
            column = jnp.where(place_ref[SECTION] == 0, column, 3 - column)
            index = lax.rem(y - step + 4, 4) * 4 + column
            for part in range(8):
                piece = refs[step][part] if depth == 0 else refs[4 + step][depth - 1, part]
                start = pl.multiple_of(index * 128 + part * 2048, 128)
                out_ref[:, pl.ds(start, 128)] = piece


def swapped(block, axis):
    return lax.ppermute(block, axis, [(0, 1), (1, 0)])


def spread(piece):
    nearest = gathered(piece, "y")
    others = jnp.stack([moved(piece, DEPTH, step) for step in (1, 2, 3)])
    return nearest + gathered(others, "y")


def reduced(near, far, awaited=None):
    rows, wide = near.shape
    block = jax.ShapeDtypeStruct((rows // 4, wide), BF)
    far = swapped(far, "c")
    if awaited is not None:
        far, awaited = lax.optimization_barrier((far, awaited))
    sums = call(add_cores, [block] * 4, (near, far), name="add_cores")
    return [moved(s, "x", 4 - step) for step, s in enumerate(sums)], awaited


def output(mirrored, attended, place, out_weight, awaited=None):
    rows, wide = attended.shape
    blocks = gathered(attended, "x")
    blocks += [swapped(b, "c") for b in blocks]
    parts = call(
        functools.partial(emit, mirrored),
        [jax.ShapeDtypeStruct((2, 8 * rows, 128), BF)] * 8,
        (place, *blocks, out_weight),
        flops=16 * rows * wide * out_weight.shape[1],
        scratch=[pltpu.VMEM((8 * rows, wide), BF)],
        name="emit",
    )
    parts = [moved(p, "y", step % 4) for step, p in enumerate(parts)]
    if awaited is not None:
        parts[0], awaited = lax.optimization_barrier((parts[0], awaited))
    share = jax.ShapeDtypeStruct((8 * rows, 128), BF)
    one, two = call(merge, [share] * 2, parts[:4], name="merge")
    received = [moved(one, DEPTH, 1), moved(two, DEPTH, 2)]
    three, own = call(merge, [share] * 2, parts[4:], name="merge")
    return [own, *received, moved(three, DEPTH, 3)], awaited


def body(hidden, query_weight, out_weight, key_cache, value_cache, cache_lengths):
    place = jnp.stack([lax.axis_index(a) for a in ("y", DEPTH, "zl", "s", "x", "c")])
    place = place.astype(jnp.int32)
    rows, wide = hidden.shape
    part = wide // 8
    place = lax.optimization_barrier(place)
    query_weight, out_weight = query_weight[0], out_weight[0]
    key = jnp.swapaxes(key_cache[0], 1, 2)
    value = jnp.swapaxes(value_cache[0], 1, 2)
    half = lax.axis_index("zl").astype(jnp.int32)
    far_index, near_index = (1 - half)[None], half[None]
    place, far_index, near_index = lax.optimization_barrier((place, far_index, near_index))
    near_half = swapped(row_half(far_index, key, value), "zl")

    sent = call(
        arrange,
        [jax.ShapeDtypeStruct((rows, part), BF)] * 8,
        (place, hidden),
        scratch=[pltpu.SemaphoreType.DMA((8,))],
        remote=(1,),
        name="arrange",
    )
    blocks = [moved(b, "x", step % 4) for step, b in enumerate(sent)]
    other = call(pick, jax.ShapeDtypeStruct((4, rows, part), BF), blocks[:4], name="pick")
    other = swapped(other, "c")
    partial = jax.ShapeDtypeStruct((4 * rows, query_weight.shape[1] + 128), BF)
    share = jax.ShapeDtypeStruct((8 * rows, 128), BF)
    held = pltpu.VMEM((8 * rows, part), BF)
    flops = 16 * rows * query_weight.shape[0] * query_weight.shape[1]
    near, far, state = call(
        project_rows,
        [partial, partial, share],
        (place, *blocks[4:], other, query_weight),
        flops=flops,
        scratch=[held],
        name="project_rows",
    )
    sums, near_half = reduced(near, far, near_half)
    query = jax.ShapeDtypeStruct((GROUP, query_weight.shape[1]), BF)
    mine, theirs = call(share_rows, [query, query], (place, *sums), name="share_rows")
    own, sent = call(
        attend_pair,
        [query, query],
        (place, cache_lengths, mine, swapped(theirs, "zl"), key, value, near_half),
        flops=8 * 8 * rows * 2048 * 256,
        name="attend_pair",
    )
    attended = call(
        rejoin,
        jax.ShapeDtypeStruct((rows, query_weight.shape[1]), BF),
        (place, own, swapped(sent, "zl")),
        name="rejoin",
    )
    near_index, attended = lax.optimization_barrier((near_index, attended))
    far_half = swapped(row_half(near_index, key, value), "zl")
    parts, far_half = output(False, attended, place, out_weight, far_half)
    first = call(merge_state, share, (*parts, state), name="merge_state")

    arrived = lax.ppermute(first, ("s", *DEPTH), [(i, 7 - i) for i in range(4)])
    near, far = call(
        project_columns,
        [partial, partial],
        (place, *spread(arrived), query_weight),
        flops=flops,
        scratch=[held],
        name="project_columns",
    )
    attended = call(
        attend,
        jax.ShapeDtypeStruct((rows, query_weight.shape[1]), BF),
        (
            place,
            cache_lengths,
            *reduced(near, far)[0],
            *(key, value, near_half, far_half),
        ),
        flops=8 * 8 * rows * 2048 * 256,
        name="attend",
    )
    parts, _ = output(True, attended, place, out_weight)
    result = call(
        merge_last,
        jax.ShapeDtypeStruct((8, rows, 128), BF),
        (place, *parts, arrived, first),
        name="merge_last",
    )
    result = lax.all_to_all(result, DP, split_axis=0, concat_axis=0, tiled=True)
    out = call(
        lay_out, jax.ShapeDtypeStruct((rows, wide), BF), (place, *spread(result)), name="lay_out"
    )
    return out[None]


def solution(mesh):
    fine = Mesh(mesh.devices.reshape(2, 4, 2, 4, 2, 2), ("s", "x", "c", "y", "zh", "zl"))
    in_specs = (
        P(DP, None),
        P("s", DP, TENSOR),
        P("s", TENSOR, DP),
        P("s", DP, None, TENSOR),
        P("s", DP, None, TENSOR),
        P(DP),
    )
    out_specs = P("s", DP, None)
    return jax.shard_map(body, mesh=fine, in_specs=in_specs, out_specs=out_specs, check_vma=False)
```

```python
import functools

import jax
import jax.numpy as jnp
from jax import lax
from jax.experimental import pallas as pl
from jax.experimental.pallas import tpu as pltpu
from jax.sharding import Mesh, PartitionSpec as P

DP = ("x", "c")
DEPTH = ("zh", "zl")
TENSOR = ("y", "zh", "zl")
BF = jnp.bfloat16
F32 = jnp.float32
VMEM = pl.BlockSpec(memory_space=pltpu.VMEM)
SMEM = pl.BlockSpec(memory_space=pltpu.SMEM)
LIMIT = 16 * 1024 * 1024
GROUP = 16
Y, Z, HALF, SECTION, X, CORE = range(6)


def call(kernel, out_shapes, args, flops=0, scratch=(), name=None):
    single = not isinstance(out_shapes, (list, tuple))
    shapes = [out_shapes] if single else list(out_shapes)
    volume = sum(a.size * a.dtype.itemsize for a in list(args) + shapes)
    return pl.pallas_call(
        kernel,
        out_shape=out_shapes,
        in_specs=[
            SMEM if a.ndim == 1 else VMEM for a in args
        ],
        out_specs=VMEM if single else [VMEM] * len(shapes),
        scratch_shapes=list(scratch),
        compiler_params=pltpu.CompilerParams(vmem_limit_bytes=LIMIT),
        cost_estimate=pl.CostEstimate(flops=flops, bytes_accessed=volume, transcendentals=0),
        name=name,
    )(*args)


def moved(block, axes, step):
    if step == 0:
        return block
    pairs = [(i, i ^ step) for i in range(lax.axis_size(axes))]
    return lax.ppermute(block, axes, pairs)


def gathered(block, axes):
    return [moved(block, axes, step) for step in range(lax.axis_size(axes))]


def arrange(place_ref, hidden_ref, *out_refs):
    x, core = place_ref[X], place_ref[CORE]
    width = out_refs[0].shape[2]
    for step, out_ref in enumerate(out_refs):
        for side in range(2):
            part = (x ^ step) * 2 + (core ^ side)
            out_ref[side] = hidden_ref[:, pl.ds(pl.multiple_of(part * width, 128), width)]


def pick(*refs):
    out_ref = refs[-1]
    for step, ref in enumerate(refs[:-1]):
        out_ref[step] = ref[1] if len(ref.shape) == 3 else ref[...]


def project(held, weight_ref, near_ref, far_ref):
    rows = near_ref.shape[0]
    width = weight_ref.shape[1]
    for start, out_ref in ((rows, far_ref), (0, near_ref)):
        wide = held[start : start + rows].astype(F32)
        squares = jnp.sum(wide * wide, axis=1, keepdims=True)
        high = squares.astype(BF).astype(F32)
        middle = (squares - high).astype(BF).astype(F32)
        low = squares - high - middle
        lane = lax.broadcasted_iota(jnp.int32, (rows, 128), 1)
        pieces = jnp.where(lane == 0, high, jnp.where(lane == 1, middle, low))
        out_ref[:, width:] = jnp.where(lane < 3, pieces, 0.0).astype(BF)

    @pl.loop(0, width // 512)
    def _(tile):
        span = pl.ds(pl.multiple_of(tile * 512, 512), 512)
        product = jnp.dot(held[...], weight_ref[:, span], preferred_element_type=F32).astype(BF)
        near_ref[:, span] = product[:rows]
        far_ref[:, span] = product[rows:]


def project_rows(place_ref, a_ref, b_ref, c_ref, d_ref, other_ref, weight_ref, *refs):
    near_ref, far_ref, state_ref, held = refs
    rows = a_ref.shape[1]
    for step, ref in enumerate((a_ref, b_ref, c_ref, d_ref)):
        held[step * rows : (step + 1) * rows] = ref[0]
        held[(step + 4) * rows : (step + 5) * rows] = other_ref[step]
    start = (place_ref[Y] * 4 + place_ref[Z]) * 128
    state_ref[...] = held[:, pl.ds(pl.multiple_of(start, 128), 128)]
    project(held, weight_ref, near_ref, far_ref)


def project_columns(place_ref, a_ref, b_ref, c_ref, d_ref, weight_ref, near_ref, far_ref, held):
    y, z = place_ref[Y], place_ref[Z]
    for step, ref in enumerate((a_ref, b_ref, c_ref, d_ref)):
        for depth in range(4):
            index = (y ^ step) * 4 + (z ^ depth ^ 3)
            held[:, pl.ds(pl.multiple_of(index * 128, 128), 128)] = ref[depth]
    project(held, weight_ref, near_ref, far_ref)


def add_cores(near_ref, far_ref, *out_refs):
    rows = out_refs[0].shape[0]
    for step, out_ref in enumerate(out_refs):
        span = slice(step * rows, (step + 1) * rows)
        out_ref[...] = (near_ref[span].astype(F32) + far_ref[span].astype(F32)).astype(BF)


def queries_of(sums, width):
    total = sums[0][...].astype(F32)
    for block in sums[1:]:
        total += block[...].astype(F32)
    squares = total[:, width : width + 1] + total[:, width + 1 : width + 2]
    squares = squares + total[:, width + 2 : width + 3]
    return total[:, :width] * lax.rsqrt(squares / 16384.0 + 1e-05)


def group_attention(half, queries, heads, lengths_ref, start, caches):
    key, key_other, value, value_other = caches
    depth, cache_len = key.shape[1:]
    count = GROUP * heads
    lane = lax.broadcasted_iota(jnp.int32, (count, 128), 1)
    row = lax.rem(lax.broadcasted_iota(jnp.int32, (count, 128), 0), GROUP)
    first = lane < 64
    side = jnp.where(first, 0, 1)
    odd = lax.rem(row, 2)

    def diagonal(block):
        return jnp.concatenate(
            [jnp.where(row == 2 * k + side, block, 0.0).astype(BF) for k in range(GROUP // 2)],
            axis=1,
        )

    def blend(values):
        product = lax.dot_general(
            probs,
            values.reshape(GROUP * depth, cache_len),
            (((1,), (1,)), ((), ())),
            preferred_element_type=F32,
        )
        result = jnp.zeros((count, 128), F32)
        for k in range(GROUP // 2):
            result += jnp.where(row // 2 == k, product[:, k * 128 : (k + 1) * 128], 0.0)
        return result

    turned = pltpu.roll(queries, 64, 1)
    low = jnp.where(first, queries, turned)
    high = jnp.where(first, turned, queries)
    own_q = jnp.where(half == 0, low, high)
    other_q = jnp.where(half == 0, high, low)
    key = key.reshape(GROUP * depth, cache_len)
    key_other = key_other.reshape(GROUP * depth, cache_len)
    scores = jnp.dot(diagonal(own_q), key, preferred_element_type=F32)
    scores += jnp.dot(diagonal(other_q), key_other, preferred_element_type=F32)
    scores = scores * (128.0**-0.5)
    limits = jnp.zeros((count, 128), jnp.int32)
    for k in range(GROUP):
        limits = jnp.where(row == k, lengths_ref[start + k], limits)
    limits = jnp.concatenate([limits] * (cache_len // 128), axis=1)
    live = lax.broadcasted_iota(jnp.int32, scores.shape, 1) < limits
    scores = jnp.where(live, scores, -1e30)
    top = jnp.max(scores, axis=1, keepdims=True)
    expd = jnp.where(live, jnp.exp(scores - top), 0.0)
    probs = (expd / jnp.sum(expd, axis=1, keepdims=True)).astype(BF)
    own = blend(value)
    other = blend(value_other)
    own = jnp.where(odd == half, own, pltpu.roll(own, 64, 1))
    other = jnp.where(odd == half, pltpu.roll(other, 64, 1), other)
    return jnp.where(side == half, own, other).astype(BF)


def stacked(block, heads):
    return jnp.concatenate([block[:, h * 128 : (h + 1) * 128] for h in range(heads)], axis=0)


def share_rows(place_ref, a_ref, b_ref, c_ref, d_ref, mine_ref, theirs_ref):
    half = place_ref[HALF]
    queries = queries_of((a_ref, b_ref, c_ref, d_ref), mine_ref.shape[1])
    top, bottom = queries[:GROUP], queries[GROUP:]
    mine_ref[...] = jnp.where(half == 0, top, bottom).astype(BF)
    theirs_ref[...] = jnp.where(half == 0, bottom, top).astype(BF)


def attend_pair(place_ref, lengths_ref, mine_ref, partner_ref, *refs):
    key_ref, value_ref, other_ref, own_ref, theirs_ref = refs
    half = place_ref[HALF]
    heads = mine_ref.shape[1] // 128
    blocks = [stacked(ref[...].astype(F32), heads) for ref in (mine_ref, partner_ref)]
    span = pl.ds(half * GROUP, GROUP)
    caches = (key_ref[span], other_ref[0], value_ref[span], other_ref[1])
    attended = group_attention(
        half, jnp.concatenate(blocks, axis=0), 2 * heads, lengths_ref, half * GROUP, caches
    )
    for index, out_ref in enumerate((own_ref, theirs_ref)):
        for h in range(heads):
            start = (index * heads + h) * GROUP
            out_ref[:, h * 128 : (h + 1) * 128] = attended[start : start + GROUP]


def rejoin(place_ref, own_ref, received_ref, out_ref):
    half = place_ref[HALF]
    top = jnp.where(half == 0, own_ref[...], received_ref[...])
    bottom = jnp.where(half == 0, received_ref[...], own_ref[...])
    for target in range(4):
        out_ref[target, :GROUP] = top
        out_ref[target, GROUP:] = bottom


def attend(place_ref, lengths_ref, a_ref, b_ref, c_ref, d_ref, *refs):
    key_ref, value_ref, near_ref, far_ref, out_ref = refs
    half = place_ref[HALF]
    heads = out_ref.shape[2] // 128
    queries = queries_of((a_ref, b_ref, c_ref, d_ref), out_ref.shape[2])

    @pl.loop(0, 2)
    def _(distance):
        index = half ^ distance
        start = pl.multiple_of(index * GROUP, GROUP)
        mine = jnp.where(index == 0, queries[:GROUP], queries[GROUP:])
        others = [jnp.where(distance == 0, near_ref[k], far_ref[k]) for k in range(2)]
        caches = (key_ref[pl.ds(start, GROUP)], others[0], value_ref[pl.ds(start, GROUP)], others[1])
        attended = group_attention(half, stacked(mine, heads), heads, lengths_ref, start, caches)
        for h in range(heads):
            tile = attended[h * GROUP : (h + 1) * GROUP]
            for target in range(4):
                out_ref[target, pl.ds(start, GROUP), h * 128 : (h + 1) * 128] = tile


def emit(mirrored, place_ref, near_ref, far_ref, weight_ref, *refs):
    out_refs, held = refs[:8], refs[8]
    y, z = place_ref[Y], place_ref[Z]
    rows = near_ref.shape[1]
    for side, ref in enumerate((near_ref, far_ref)):
        for step in range(4):
            start = (4 * side + step) * rows
            held[start : start + rows] = ref[place_ref[X] ^ step]
    for half, depths in enumerate(((1, 2), (3, 0))):
        for step in range(4):
            columns = []
            for depth in depths:
                column = z ^ depth ^ 3 if mirrored else z ^ depth
                start = pl.multiple_of(((y ^ step) * 4 + column) * 128, 128)
                columns.append(weight_ref[:, pl.ds(start, 128)])
            product = jnp.dot(
                held[...], jnp.concatenate(columns, axis=1), preferred_element_type=F32
            ).astype(BF)
            out_refs[4 * half + step][0] = product[:, :128]
            out_refs[4 * half + step][1] = product[:, 128:]


def merge(*refs):
    sources, targets = refs[:4], refs[4:]
    for index, target in enumerate(targets):
        total = sources[0][index].astype(F32)
        for source in sources[1:]:
            total += source[index].astype(F32)
        target[...] = total.astype(BF)


def updated(sources, state):
    total = sources[0][...].astype(F32)
    for source in sources[1:]:
        total += source[...].astype(F32)
    total = total.astype(BF).astype(F32)
    return (state.astype(F32) + total).astype(BF)


def merge_state(*refs):
    sources, state_ref, out_ref = refs[:4], refs[4], refs[5]
    out_ref[...] = updated(sources, state_ref[...])


def merge_last(place_ref, *refs):
    sources, state_ref, first_ref, out_ref = refs[:4], refs[4], refs[5], refs[6]
    result = updated(sources, state_ref[...]).astype(F32)
    result = jnp.where(place_ref[SECTION] == 0, first_ref[...].astype(F32), result).astype(BF)
    rows = out_ref.shape[1]
    for side in range(2):
        for step in range(4):
            owner = (place_ref[X] ^ step) * 2 + (place_ref[CORE] ^ side)
            start = (side * 4 + step) * rows
            out_ref[owner] = result[start : start + rows]


def lay_out(place_ref, *refs):
    y, z = place_ref[Y], place_ref[Z]
    out_ref = refs[-1]
    mirror = jnp.where(place_ref[SECTION] == 0, 0, 3)
    for step, ref in enumerate(refs[:-1]):
        for depth in range(4):
            index = (y ^ step) * 4 + (z ^ depth ^ mirror)
            for part in range(8):
                start = pl.multiple_of(index * 128 + part * 2048, 128)
                out_ref[:, pl.ds(start, 128)] = ref[depth, part]


def row_half(index, key, value):
    halves = [
        lax.dynamic_index_in_dim(c.reshape(2, GROUP, *c.shape[1:]), index, 0, keepdims=False)
        for c in (key, value)
    ]
    return jnp.stack(halves)


def spread(piece):
    return gathered(jnp.stack(gathered(piece, DEPTH)), "y")


def reduced(near, far):
    rows, wide = near.shape
    block = jax.ShapeDtypeStruct((rows // 4, wide), BF)
    sums = call(add_cores, [block] * 4, (near, moved(far, "c", 1)), name="add_cores")
    return [moved(s, "x", step) for step, s in enumerate(sums)]


def traded(blocks, axes):
    return lax.all_to_all(blocks, axes, split_axis=0, concat_axis=0, tiled=True)


def output(mirrored, attended, place, out_weight, awaited=None):
    near = traded(attended, "x")
    rows, wide = 8 * near.shape[1], near.shape[2]
    parts = call(
        functools.partial(emit, mirrored),
        [jax.ShapeDtypeStruct((2, rows, 128), BF)] * 8,
        (place, near, moved(near, "c", 1), out_weight),
        flops=2 * rows * wide * out_weight.shape[1],
        scratch=[pltpu.VMEM((rows, wide), BF)],
        name="emit",
    )
    parts = [moved(p, "y", step % 4) for step, p in enumerate(parts)]
    if awaited is not None:
        parts[4], awaited = lax.optimization_barrier((parts[4], awaited))
    share = jax.ShapeDtypeStruct((rows, 128), BF)
    one, two = call(merge, [share] * 2, parts[:4], name="merge")
    received = [moved(one, DEPTH, 1), moved(two, DEPTH, 2)]
    three, own = call(merge, [share] * 2, parts[4:], name="merge")
    return [own, *received, moved(three, DEPTH, 3)], awaited


def body(hidden, query_weight, out_weight, key_cache, value_cache, cache_lengths):
    place = jnp.stack([lax.axis_index(a) for a in ("y", DEPTH, "zl", "s", "x", "c")])
    place = place.astype(jnp.int32)
    rows, wide = hidden.shape
    part = wide // 8
    place = lax.optimization_barrier(place)
    query_weight, out_weight = query_weight[0], out_weight[0]
    key = jnp.swapaxes(key_cache[0], 1, 2)
    value = jnp.swapaxes(value_cache[0], 1, 2)
    half = lax.axis_index("zl").astype(jnp.int32)
    place, half = lax.optimization_barrier((place, half))
    near_half = moved(row_half(1 - half, key, value), "zl", 1)
    sent = call(
        arrange,
        [jax.ShapeDtypeStruct((2, rows, part), BF)] * 4,
        (place, hidden),
        name="arrange",
    )
    blocks = [moved(b, "x", step) for step, b in enumerate(sent)]
    other = call(pick, jax.ShapeDtypeStruct((4, rows, part), BF), blocks, name="pick")
    other = moved(other, "c", 1)
    partial = jax.ShapeDtypeStruct((4 * rows, query_weight.shape[1] + 128), BF)
    share = jax.ShapeDtypeStruct((8 * rows, 128), BF)
    held = pltpu.VMEM((8 * rows, part), BF)
    flops = 16 * rows * query_weight.shape[0] * query_weight.shape[1]
    near, far, state = call(
        project_rows,
        [partial, partial, share],
        (place, *blocks, other, query_weight),
        flops=flops,
        scratch=[held],
        name="project_rows",
    )
    far, near_half = lax.optimization_barrier((far, near_half))
    sums = reduced(near, far)
    query = jax.ShapeDtypeStruct((GROUP, query_weight.shape[1]), BF)
    mine, theirs = call(share_rows, [query, query], (place, *sums), name="share_rows")
    copies = jax.ShapeDtypeStruct((4, rows, query_weight.shape[1]), BF)
    own, sent = call(
        attend_pair,
        [query, query],
        (place, cache_lengths, mine, moved(theirs, "zl", 1), key, value, near_half),
        flops=8 * 8 * rows * 2048 * 256,
        name="attend_pair",
    )
    attended = call(
        rejoin,
        copies,
        (place, own, moved(sent, "zl", 1)),
        name="rejoin",
    )
    half, attended = lax.optimization_barrier((half, attended))
    far_half = moved(row_half(half, key, value), "zl", 1)
    parts, far_half = output(False, attended, place, out_weight, far_half)
    first = call(merge_state, share, (*parts, state), name="merge_state")

    arrived = moved(first, ("s", *DEPTH), 7)
    near, far = call(
        project_columns,
        [partial, partial],
        (place, *spread(arrived), query_weight),
        flops=flops,
        scratch=[held],
        name="project_columns",
    )
    attended = call(
        attend,
        copies,
        (
            place,
            cache_lengths,
            *reduced(near, far),
            *(key, value, near_half, far_half),
        ),
        flops=8 * 8 * rows * 2048 * 256,
        name="attend",
    )
    parts, _ = output(True, attended, place, out_weight)
    result = call(
        merge_last,
        jax.ShapeDtypeStruct((8, rows, 128), BF),
        (place, *parts, arrived, first),
        name="merge_last",
    )
    result = traded(result, DP)
    out = call(
        lay_out, jax.ShapeDtypeStruct((rows, wide), BF), (place, *spread(result)), name="lay_out"
    )
    return out[None]


def solution(mesh):
    fine = Mesh(mesh.devices.reshape(2, 4, 2, 4, 2, 2), ("s", "x", "c", "y", "zh", "zl"))
    in_specs = (
        P(DP, None),
        P("s", DP, TENSOR),
        P("s", TENSOR, DP),
        P("s", DP, None, TENSOR),
        P("s", DP, None, TENSOR),
        P(DP),
    )
    out_specs = P("s", DP, None)
    return jax.shard_map(body, mesh=fine, in_specs=in_specs, out_specs=out_specs, check_vma=False)
```

```python
import functools

import jax
import jax.numpy as jnp
from jax import lax
from jax.experimental import pallas as pl
from jax.experimental.pallas import tpu as pltpu
from jax.sharding import Mesh, PartitionSpec as P

DP = ("x", "c")
DEPTH = ("zh", "zl")
TENSOR = ("y", "zh", "zl")
BF = jnp.bfloat16
F32 = jnp.float32
VMEM = pl.BlockSpec(memory_space=pltpu.VMEM)
SMEM = pl.BlockSpec(memory_space=pltpu.SMEM)
LIMIT = 16 * 1024 * 1024
GROUP = 16
Y, Z, HALF, SECTION, X, CORE = range(6)


def call(kernel, out_shapes, args, flops=0, scratch=(), name=None):
    single = not isinstance(out_shapes, (list, tuple))
    shapes = [out_shapes] if single else list(out_shapes)
    volume = sum(a.size * a.dtype.itemsize for a in list(args) + shapes)
    return pl.pallas_call(
        kernel,
        out_shape=out_shapes,
        in_specs=[
            SMEM if a.ndim == 1 else VMEM for a in args
        ],
        out_specs=VMEM if single else [VMEM] * len(shapes),
        scratch_shapes=list(scratch),
        compiler_params=pltpu.CompilerParams(vmem_limit_bytes=LIMIT),
        cost_estimate=pl.CostEstimate(flops=flops, bytes_accessed=volume, transcendentals=0),
        name=name,
    )(*args)


def moved(block, axes, step):
    if step == 0:
        return block
    pairs = [(i, i ^ step) for i in range(lax.axis_size(axes))]
    return lax.ppermute(block, axes, pairs)


def gathered(block, axes):
    return [moved(block, axes, step) for step in range(lax.axis_size(axes))]


def arrange(place_ref, hidden_ref, *out_refs):
    x, core = place_ref[X], place_ref[CORE]
    width = out_refs[0].shape[2]
    for step, out_ref in enumerate(out_refs):
        for side in range(2):
            part = (x ^ step) * 2 + (core ^ side)
            out_ref[side] = hidden_ref[:, pl.ds(pl.multiple_of(part * width, 128), width)]


def pick(*refs):
    out_ref = refs[-1]
    for step, ref in enumerate(refs[:-1]):
        out_ref[step] = ref[1] if len(ref.shape) == 3 else ref[...]


def project(held, weight_ref, near_ref, far_ref):
    rows = near_ref.shape[0]
    width = weight_ref.shape[1]
    for start, out_ref in ((rows, far_ref), (0, near_ref)):
        wide = held[start : start + rows].astype(F32)
        squares = jnp.sum(wide * wide, axis=1, keepdims=True)
        high = squares.astype(BF).astype(F32)
        middle = (squares - high).astype(BF).astype(F32)
        low = squares - high - middle
        lane = lax.broadcasted_iota(jnp.int32, (rows, 128), 1)
        pieces = jnp.where(lane == 0, high, jnp.where(lane == 1, middle, low))
        out_ref[:, width:] = jnp.where(lane < 3, pieces, 0.0).astype(BF)

    for tile in range(width // 256):
        span = slice(tile * 256, (tile + 1) * 256)
        product = jnp.dot(held[...], weight_ref[:, span], preferred_element_type=F32).astype(BF)
        near_ref[:, span] = product[:rows]
        far_ref[:, span] = product[rows:]


def project_rows(place_ref, a_ref, b_ref, c_ref, d_ref, other_ref, weight_ref, *refs):
    near_ref, far_ref, state_ref, held = refs
    rows = a_ref.shape[1]
    for step, ref in enumerate((a_ref, b_ref, c_ref, d_ref)):
        held[step * rows : (step + 1) * rows] = ref[0]
        held[(step + 4) * rows : (step + 5) * rows] = other_ref[step]
    start = (place_ref[Y] * 4 + place_ref[Z]) * 128
    state_ref[...] = held[:, pl.ds(pl.multiple_of(start, 128), 128)]
    project(held, weight_ref, near_ref, far_ref)


def project_columns(place_ref, a_ref, b_ref, c_ref, d_ref, weight_ref, near_ref, far_ref, held):
    y, z = place_ref[Y], place_ref[Z]
    for step, ref in enumerate((a_ref, b_ref, c_ref, d_ref)):
        for depth in range(4):
            index = (y ^ step) * 4 + (z ^ depth ^ 3)
            held[:, pl.ds(pl.multiple_of(index * 128, 128), 128)] = ref[depth]
    project(held, weight_ref, near_ref, far_ref)


def add_cores(near_ref, far_ref, *out_refs):
    rows = out_refs[0].shape[0]
    for step, out_ref in enumerate(out_refs):
        span = slice(step * rows, (step + 1) * rows)
        out_ref[...] = (near_ref[span].astype(F32) + far_ref[span].astype(F32)).astype(BF)


def add_cores_pair(place_ref, near_ref, far_ref, out_ref):
    for step in range(4):
        for part in range(2):
            start = (2 * step + part) * GROUP
            span = slice(start, start + GROUP)
            total = near_ref[span].astype(F32) + far_ref[span].astype(F32)
            out_ref[(place_ref[X] ^ step) * 2 + part] = total.astype(BF)


def queries_of(sums, width):
    total = sums[0].astype(F32)
    for block in sums[1:]:
        total += block.astype(F32)
    squares = total[:, width : width + 1] + total[:, width + 1 : width + 2]
    squares = squares + total[:, width + 2 : width + 3]
    return total[:, :width] * lax.rsqrt(squares / 16384.0 + 1e-05)


def group_attention(half, queries, heads, lengths_ref, start, caches):
    key, key_other, value, value_other = caches
    depth, cache_len = key.shape[1:]
    count = GROUP * heads
    lane = lax.broadcasted_iota(jnp.int32, (count, 128), 1)
    row = lax.rem(lax.broadcasted_iota(jnp.int32, (count, 128), 0), GROUP)
    first = lane < 64
    side = jnp.where(first, 0, 1)
    odd = lax.rem(row, 2)

    def diagonal(block):
        return jnp.concatenate(
            [jnp.where(row == 2 * k + side, block, 0.0).astype(BF) for k in range(GROUP // 2)],
            axis=1,
        )

    def blend(values):
        product = lax.dot_general(
            probs,
            values.reshape(GROUP * depth, cache_len),
            (((1,), (1,)), ((), ())),
            preferred_element_type=F32,
        )
        result = jnp.zeros((count, 128), F32)
        for k in range(GROUP // 2):
            result += jnp.where(row // 2 == k, product[:, k * 128 : (k + 1) * 128], 0.0)
        return result

    turned = pltpu.roll(queries, 64, 1)
    low = jnp.where(first, queries, turned)
    high = jnp.where(first, turned, queries)
    own_q = jnp.where(half == 0, low, high)
    other_q = jnp.where(half == 0, high, low)
    key = key.reshape(GROUP * depth, cache_len)
    key_other = key_other.reshape(GROUP * depth, cache_len)
    scores = jnp.dot(diagonal(own_q), key, preferred_element_type=F32)
    scores += jnp.dot(diagonal(other_q), key_other, preferred_element_type=F32)
    scores = scores * (128.0**-0.5)
    limits = jnp.zeros((count, 128), jnp.int32)
    for k in range(GROUP):
        limits = jnp.where(row == k, lengths_ref[start + k], limits)
    limits = jnp.concatenate([limits] * (cache_len // 128), axis=1)
    live = lax.broadcasted_iota(jnp.int32, scores.shape, 1) < limits
    scores = jnp.where(live, scores, -1e30)
    top = jnp.max(scores, axis=1, keepdims=True)
    expd = jnp.where(live, jnp.exp(scores - top), 0.0)
    probs = (expd / jnp.sum(expd, axis=1, keepdims=True)).astype(BF)
    own = blend(value)
    other = blend(value_other)
    own = jnp.where(odd == half, own, pltpu.roll(own, 64, 1))
    other = jnp.where(odd == half, pltpu.roll(other, 64, 1), other)
    return jnp.where(side == half, own, other).astype(BF)


def stacked(block, heads):
    return jnp.concatenate([block[:, h * 128 : (h + 1) * 128] for h in range(heads)], axis=0)


def attend_pair(place_ref, lengths_ref, sums_ref, key_ref, value_ref, other_ref, out_ref):
    half = place_ref[HALF]
    width = out_ref.shape[2]
    heads = width // 128
    parts = [
        queries_of([sums_ref[2 * source + part] for source in range(4)], width) for part in range(2)
    ]
    blocks = [stacked(part, heads) for part in parts]
    caches = (key_ref[...], other_ref[0], value_ref[...], other_ref[1])
    attended = group_attention(
        half, jnp.concatenate(blocks, axis=0), 2 * heads, lengths_ref, half * GROUP, caches
    )
    for part in range(2):
        for h in range(heads):
            start = (part * heads + h) * GROUP
            for target in range(4):
                out_ref[2 * target + part, :, h * 128 : (h + 1) * 128] = attended[
                    start : start + GROUP
                ]


def attend(place_ref, lengths_ref, a_ref, b_ref, c_ref, d_ref, *refs):
    key_ref, value_ref, near_ref, far_key_ref, far_value_ref, out_ref = refs
    half = place_ref[HALF]
    heads = out_ref.shape[2] // 128
    sums = [ref[...] for ref in (a_ref, b_ref, c_ref, d_ref)]
    queries = queries_of(sums, out_ref.shape[2])

    @pl.loop(0, 2)
    def _(distance):
        index = half ^ distance
        start = pl.multiple_of(index * GROUP, GROUP)
        mine = jnp.where(index == 0, queries[:GROUP], queries[GROUP:])
        other_key = jnp.where(distance == 0, near_ref[0], far_key_ref[...])
        other_value = jnp.where(distance == 0, near_ref[1], far_value_ref[...])
        span = pl.ds(start, GROUP)
        caches = (key_ref[span], other_key, value_ref[span], other_value)
        attended = group_attention(half, stacked(mine, heads), heads, lengths_ref, start, caches)
        for h in range(heads):
            tile = attended[h * GROUP : (h + 1) * GROUP]
            for target in range(4):
                out_ref[target, pl.ds(start, GROUP), h * 128 : (h + 1) * 128] = tile


def emit(mirrored, place_ref, near_ref, far_ref, weight_ref, *refs):
    out_refs, held = refs[:8], refs[8]
    y, z = place_ref[Y], place_ref[Z]
    rows = near_ref.shape[1]
    for side, ref in enumerate((near_ref, far_ref)):
        for step in range(4):
            start = (4 * side + step) * rows
            held[start : start + rows] = ref[place_ref[X] ^ step]
    for half, depths in enumerate(((1, 2), (3, 0))):
        for step in range(4):
            columns = []
            for depth in depths:
                column = z ^ depth ^ 3 if mirrored else z ^ depth
                start = pl.multiple_of(((y ^ step) * 4 + column) * 128, 128)
                columns.append(weight_ref[:, pl.ds(start, 128)])
            product = jnp.dot(
                held[...], jnp.concatenate(columns, axis=1), preferred_element_type=F32
            ).astype(BF)
            out_refs[4 * half + step][0] = product[:, :128]
            out_refs[4 * half + step][1] = product[:, 128:]


def merge(*refs):
    sources, targets = refs[:4], refs[4:]
    for index, target in enumerate(targets):
        total = sources[0][index].astype(F32)
        for source in sources[1:]:
            total += source[index].astype(F32)
        target[...] = total.astype(BF)


def updated(sources, state):
    total = sources[0][...].astype(F32)
    for source in sources[1:]:
        total += source[...].astype(F32)
    total = total.astype(BF).astype(F32)
    return (state.astype(F32) + total).astype(BF)


def merge_state(*refs):
    sources, state_ref, out_ref = refs[:4], refs[4], refs[5]
    out_ref[...] = updated(sources, state_ref[...])


def merge_last(place_ref, *refs):
    sources, state_ref, first_ref, out_ref = refs[:4], refs[4], refs[5], refs[6]
    result = updated(sources, state_ref[...]).astype(F32)
    result = jnp.where(place_ref[SECTION] == 0, first_ref[...].astype(F32), result).astype(BF)
    rows = out_ref.shape[1]
    for side in range(2):
        for step in range(4):
            owner = (place_ref[X] ^ step) * 2 + (place_ref[CORE] ^ side)
            start = (side * 4 + step) * rows
            out_ref[owner] = result[start : start + rows]


def lay_out(place_ref, *refs):
    y, z = place_ref[Y], place_ref[Z]
    out_ref = refs[-1]
    mirror = jnp.where(place_ref[SECTION] == 0, 0, 3)
    for step, ref in enumerate(refs[:-1]):
        for depth in range(4):
            index = (y ^ step) * 4 + (z ^ depth ^ mirror)
            for part in range(8):
                start = pl.multiple_of(index * 128 + part * 2048, 128)
                out_ref[:, pl.ds(start, 128)] = ref[depth, part]


def row_half(index, cache):
    halves = cache.reshape(2, GROUP, *cache.shape[1:])
    return lax.dynamic_index_in_dim(halves, index, 0, keepdims=False)


def spread(piece):
    return gathered(jnp.stack(gathered(piece, DEPTH)), "y")


def reduced(near, far):
    rows, wide = near.shape
    block = jax.ShapeDtypeStruct((rows // 4, wide), BF)
    sums = call(add_cores, [block] * 4, (near, moved(far, "c", 1)), name="add_cores")
    return [moved(s, "x", step) for step, s in enumerate(sums)]


def traded(blocks, axes):
    return lax.all_to_all(blocks, axes, split_axis=0, concat_axis=0, tiled=True)


def output(mirrored, near, place, out_weight, awaited=None):
    rows, wide = 8 * near.shape[1], near.shape[2]
    parts = call(
        functools.partial(emit, mirrored),
        [jax.ShapeDtypeStruct((2, rows, 128), BF)] * 8,
        (place, near, moved(near, "c", 1), out_weight),
        flops=2 * rows * wide * out_weight.shape[1],
        scratch=[pltpu.VMEM((rows, wide), BF)],
        name="emit",
    )
    parts = [moved(p, "y", step % 4) for step, p in enumerate(parts)]
    if awaited is not None:
        parts[0], awaited = lax.optimization_barrier((parts[0], awaited))
    share = jax.ShapeDtypeStruct((rows, 128), BF)
    one, two = call(merge, [share] * 2, parts[:4], name="merge")
    received = [moved(one, DEPTH, 1), moved(two, DEPTH, 2)]
    three, own = call(merge, [share] * 2, parts[4:], name="merge")
    return [own, *received, moved(three, DEPTH, 3)], awaited


def body(hidden, query_weight, out_weight, key_cache, value_cache, cache_lengths):
    place = jnp.stack([lax.axis_index(a) for a in ("y", DEPTH, "zl", "s", "x", "c")])
    place = place.astype(jnp.int32)
    rows, wide = hidden.shape
    part = wide // 8
    place = lax.optimization_barrier(place)
    query_weight, out_weight = query_weight[0], out_weight[0]
    key = jnp.swapaxes(key_cache[0], 1, 2)
    value = jnp.swapaxes(value_cache[0], 1, 2)
    half = lax.axis_index("zl").astype(jnp.int32)
    place, half = lax.optimization_barrier((place, half))
    near_half = jnp.stack([row_half(1 - half, key), row_half(1 - half, value)])
    near_half = moved(near_half, "zl", 1)
    sent = call(
        arrange,
        [jax.ShapeDtypeStruct((2, rows, part), BF)] * 4,
        (place, hidden),
        name="arrange",
    )
    blocks = [moved(b, "x", step) for step, b in enumerate(sent)]
    mine_key, mine_value = row_half(half, key), row_half(half, value)
    mine_key, mine_value, blocks[1] = lax.optimization_barrier((mine_key, mine_value, blocks[1]))
    other = call(pick, jax.ShapeDtypeStruct((4, rows, part), BF), blocks, name="pick")
    other = moved(other, "c", 1)
    partial = jax.ShapeDtypeStruct((4 * rows, query_weight.shape[1] + 128), BF)
    share = jax.ShapeDtypeStruct((8 * rows, 128), BF)
    held = pltpu.VMEM((8 * rows, part), BF)
    flops = 16 * rows * query_weight.shape[0] * query_weight.shape[1]
    near, far, state = call(
        project_rows,
        [partial, partial, share],
        (place, *blocks, other, query_weight),
        flops=flops,
        scratch=[held],
        name="project_rows",
    )
    far, near_half = lax.optimization_barrier((far, near_half))
    width = query_weight.shape[1]
    sums = call(
        add_cores_pair,
        jax.ShapeDtypeStruct((8, GROUP, width + 128), BF),
        (place, near, moved(far, "c", 1)),
        name="add_cores_pair",
    )
    attended = call(
        attend_pair,
        jax.ShapeDtypeStruct((8, GROUP, width), BF),
        (place, cache_lengths, traded(sums, ("x", "zl")), mine_key, mine_value, near_half),
        flops=8 * 8 * rows * 2048 * 256,
        name="attend_pair",
    )
    attended = traded(attended, ("x", "zl")).reshape(4, rows, width)
    mine_key, attended = lax.optimization_barrier((mine_key, attended))
    far_key = moved(mine_key, "zl", 1)
    parts, far_key = output(False, attended, place, out_weight, far_key)
    first = call(merge_state, share, (*parts, state), name="merge_state")

    arrived = moved(first, ("s", *DEPTH), 7)
    chunk = jnp.stack(gathered(arrived, DEPTH))
    chunk, mine_value = lax.optimization_barrier((chunk, mine_value))
    chunks = gathered(chunk, "y")
    far_value = moved(mine_value, "zl", 1)
    near, far = call(
        project_columns,
        [partial, partial],
        (place, *chunks, query_weight),
        flops=flops,
        scratch=[held],
        name="project_columns",
    )
    attended = call(
        attend,
        jax.ShapeDtypeStruct((4, rows, width), BF),
        (
            place,
            cache_lengths,
            *reduced(near, far),
            *(key, value, near_half, far_key, far_value),
        ),
        flops=8 * 8 * rows * 2048 * 256,
        name="attend",
    )
    parts, _ = output(True, traded(attended, "x"), place, out_weight)
    result = call(
        merge_last,
        jax.ShapeDtypeStruct((8, rows, 128), BF),
        (place, *parts, arrived, first),
        name="merge_last",
    )
    result = traded(result, DP)
    out = call(
        lay_out, jax.ShapeDtypeStruct((rows, wide), BF), (place, *spread(result)), name="lay_out"
    )
    return out[None]


def solution(mesh):
    fine = Mesh(mesh.devices.reshape(2, 4, 2, 4, 2, 2), ("s", "x", "c", "y", "zh", "zl"))
    in_specs = (
        P(DP, None),
        P("s", DP, TENSOR),
        P("s", TENSOR, DP),
        P("s", DP, None, TENSOR),
        P("s", DP, None, TENSOR),
        P(DP),
    )
    out_specs = P("s", DP, None)
    return jax.shard_map(body, mesh=fine, in_specs=in_specs, out_specs=out_specs, check_vma=False)
```

```python
import functools

import jax
import jax.numpy as jnp
from jax import lax
from jax.experimental import pallas as pl
from jax.experimental.pallas import tpu as pltpu
from jax.sharding import Mesh, PartitionSpec as P

DP = ("x", "c")
DEPTH = ("zh", "zl")
TENSOR = ("y", "zh", "zl")
BF = jnp.bfloat16
F32 = jnp.float32
VMEM = pl.BlockSpec(memory_space=pltpu.VMEM)
SMEM = pl.BlockSpec(memory_space=pltpu.SMEM)
LIMIT = 16 * 1024 * 1024
GROUP = 16
Y, Z, HALF, SECTION, X, CORE = range(6)


def call(kernel, out_shapes, args, flops=0, scratch=(), name=None):
    single = not isinstance(out_shapes, (list, tuple))
    shapes = [out_shapes] if single else list(out_shapes)
    volume = sum(a.size * a.dtype.itemsize for a in list(args) + shapes)
    return pl.pallas_call(
        kernel,
        out_shape=out_shapes,
        in_specs=[
            SMEM if a.ndim == 1 else VMEM for a in args
        ],
        out_specs=VMEM if single else [VMEM] * len(shapes),
        scratch_shapes=list(scratch),
        compiler_params=pltpu.CompilerParams(vmem_limit_bytes=LIMIT),
        cost_estimate=pl.CostEstimate(flops=flops, bytes_accessed=volume, transcendentals=0),
        name=name,
    )(*args)


def moved(block, axes, step):
    if step == 0:
        return block
    pairs = [(i, i ^ step) for i in range(lax.axis_size(axes))]
    return lax.ppermute(block, axes, pairs)


def gathered(block, axes):
    return [moved(block, axes, step) for step in range(lax.axis_size(axes))]


def arrange(place_ref, hidden_ref, *out_refs):
    x, core = place_ref[X], place_ref[CORE]
    width = out_refs[0].shape[2]
    for step, out_ref in enumerate(out_refs):
        for side in range(2):
            part = (x ^ step) * 2 + (core ^ side)
            out_ref[side] = hidden_ref[:, pl.ds(pl.multiple_of(part * width, 128), width)]


def pick(*refs):
    out_ref = refs[-1]
    for step, ref in enumerate(refs[:-1]):
        out_ref[step] = ref[1] if len(ref.shape) == 3 else ref[...]


def project(held, weight_ref, near_ref, far_ref, unrolled):
    rows = near_ref.shape[0]
    width = weight_ref.shape[1]
    for start, out_ref in ((rows, far_ref), (0, near_ref)):
        wide = held[start : start + rows].astype(F32)
        squares = jnp.sum(wide * wide, axis=1, keepdims=True)
        high = squares.astype(BF).astype(F32)
        middle = (squares - high).astype(BF).astype(F32)
        low = squares - high - middle
        lane = lax.broadcasted_iota(jnp.int32, (rows, 128), 1)
        pieces = jnp.where(lane == 0, high, jnp.where(lane == 1, middle, low))
        out_ref[:, width:] = jnp.where(lane < 3, pieces, 0.0).astype(BF)

    def multiply(span):
        product = jnp.dot(held[...], weight_ref[:, span], preferred_element_type=F32).astype(BF)
        near_ref[:, span] = product[:rows]
        far_ref[:, span] = product[rows:]

    if unrolled:
        for start in range(0, width, 256):
            multiply(slice(start, start + 256))
        return

    @pl.loop(0, width // 512)
    def _(tile):
        multiply(pl.ds(pl.multiple_of(tile * 512, 512), 512))


def project_rows(place_ref, a_ref, b_ref, c_ref, d_ref, other_ref, weight_ref, *refs):
    near_ref, far_ref, state_ref, held = refs
    rows = a_ref.shape[1]
    for step, ref in enumerate((a_ref, b_ref, c_ref, d_ref)):
        held[step * rows : (step + 1) * rows] = ref[0]
        held[(step + 4) * rows : (step + 5) * rows] = other_ref[step]
    start = (place_ref[Y] * 4 + place_ref[Z]) * 128
    state_ref[...] = held[:, pl.ds(pl.multiple_of(start, 128), 128)]
    project(held, weight_ref, near_ref, far_ref, False)


def project_columns(place_ref, a_ref, b_ref, c_ref, d_ref, weight_ref, near_ref, far_ref, held):
    y, z = place_ref[Y], place_ref[Z]
    for step, ref in enumerate((a_ref, b_ref, c_ref, d_ref)):
        for depth in range(4):
            index = (y ^ step) * 4 + (z ^ depth ^ 3)
            held[:, pl.ds(pl.multiple_of(index * 128, 128), 128)] = ref[depth]
    project(held, weight_ref, near_ref, far_ref, True)


def add_cores(near_ref, far_ref, *out_refs):
    rows = out_refs[0].shape[0]
    for step, out_ref in enumerate(out_refs):
        span = slice(step * rows, (step + 1) * rows)
        out_ref[...] = (near_ref[span].astype(F32) + far_ref[span].astype(F32)).astype(BF)


def add_cores_pair(place_ref, near_ref, far_ref, out_ref):
    for step in range(4):
        for part in range(2):
            start = (2 * step + part) * GROUP
            span = slice(start, start + GROUP)
            total = near_ref[span].astype(F32) + far_ref[span].astype(F32)
            out_ref[(place_ref[X] ^ step) * 2 + part] = total.astype(BF)


def queries_of(sums, width):
    total = sums[0].astype(F32)
    for block in sums[1:]:
        total += block.astype(F32)
    squares = total[:, width : width + 1] + total[:, width + 1 : width + 2]
    squares = squares + total[:, width + 2 : width + 3]
    return total[:, :width] * lax.rsqrt(squares / 16384.0 + 1e-05)


def group_attention(half, queries, heads, lengths_ref, start, caches):
    key, key_other, value, value_other = caches
    depth, cache_len = key.shape[1:]
    count = GROUP * heads
    lane = lax.broadcasted_iota(jnp.int32, (count, 128), 1)
    row = lax.rem(lax.broadcasted_iota(jnp.int32, (count, 128), 0), GROUP)
    first = lane < 64
    side = jnp.where(first, 0, 1)
    odd = lax.rem(row, 2)

    def diagonal(block):
        return jnp.concatenate(
            [jnp.where(row == 2 * k + side, block, 0.0).astype(BF) for k in range(GROUP // 2)],
            axis=1,
        )

    def blend(values):
        product = lax.dot_general(
            probs,
            values.reshape(GROUP * depth, cache_len),
            (((1,), (1,)), ((), ())),
            preferred_element_type=F32,
        )
        result = jnp.zeros((count, 128), F32)
        for k in range(GROUP // 2):
            result += jnp.where(row // 2 == k, product[:, k * 128 : (k + 1) * 128], 0.0)
        return result

    turned = pltpu.roll(queries, 64, 1)
    low = jnp.where(first, queries, turned)
    high = jnp.where(first, turned, queries)
    own_q = jnp.where(half == 0, low, high)
    other_q = jnp.where(half == 0, high, low)
    key = key.reshape(GROUP * depth, cache_len)
    key_other = key_other.reshape(GROUP * depth, cache_len)
    scores = jnp.dot(diagonal(own_q), key, preferred_element_type=F32)
    scores += jnp.dot(diagonal(other_q), key_other, preferred_element_type=F32)
    scores = scores * (128.0**-0.5)
    limits = jnp.zeros((count, 128), jnp.int32)
    for k in range(GROUP):
        limits = jnp.where(row == k, lengths_ref[start + k], limits)
    limits = jnp.concatenate([limits] * (cache_len // 128), axis=1)
    live = lax.broadcasted_iota(jnp.int32, scores.shape, 1) < limits
    scores = jnp.where(live, scores, -1e30)
    top = jnp.max(scores, axis=1, keepdims=True)
    expd = jnp.where(live, jnp.exp(scores - top), 0.0)
    probs = (expd / jnp.sum(expd, axis=1, keepdims=True)).astype(BF)
    own = blend(value)
    other = blend(value_other)
    own = jnp.where(odd == half, own, pltpu.roll(own, 64, 1))
    other = jnp.where(odd == half, pltpu.roll(other, 64, 1), other)
    return jnp.where(side == half, own, other).astype(BF)


def stacked(block, heads):
    return jnp.concatenate([block[:, h * 128 : (h + 1) * 128] for h in range(heads)], axis=0)


def attend_pair(place_ref, lengths_ref, sums_ref, key_ref, value_ref, other_ref, out_ref):
    half = place_ref[HALF]
    width = out_ref.shape[2]
    heads = width // 128
    parts = [
        queries_of([sums_ref[2 * source + part] for source in range(4)], width) for part in range(2)
    ]
    blocks = [stacked(part, heads) for part in parts]
    caches = (key_ref[...], other_ref[0], value_ref[...], other_ref[1])
    attended = group_attention(
        half, jnp.concatenate(blocks, axis=0), 2 * heads, lengths_ref, half * GROUP, caches
    )
    for part in range(2):
        for h in range(heads):
            start = (part * heads + h) * GROUP
            for target in range(4):
                out_ref[2 * target + part, :, h * 128 : (h + 1) * 128] = attended[
                    start : start + GROUP
                ]


def attend(place_ref, lengths_ref, a_ref, b_ref, c_ref, d_ref, *refs):
    key_ref, value_ref, near_ref, far_key_ref, far_value_ref, out_ref = refs
    half = place_ref[HALF]
    heads = out_ref.shape[1] // 128
    sums = [ref[...] for ref in (a_ref, b_ref, c_ref, d_ref)]
    queries = queries_of(sums, out_ref.shape[1])

    @pl.loop(0, 2)
    def _(distance):
        index = half ^ distance
        start = pl.multiple_of(index * GROUP, GROUP)
        mine = jnp.where(index == 0, queries[:GROUP], queries[GROUP:])
        other_key = jnp.where(distance == 0, near_ref[0], far_key_ref[...])
        other_value = jnp.where(distance == 0, near_ref[1], far_value_ref[...])
        span = pl.ds(start, GROUP)
        caches = (key_ref[span], other_key, value_ref[span], other_value)
        attended = group_attention(half, stacked(mine, heads), heads, lengths_ref, start, caches)
        for h in range(heads):
            tile = attended[h * GROUP : (h + 1) * GROUP]
            out_ref[pl.ds(start, GROUP), h * 128 : (h + 1) * 128] = tile


def emit(mirrored, place_ref, near_ref, far_ref, weight_ref, *refs):
    out_refs, held = refs[:8], refs[8]
    y, z = place_ref[Y], place_ref[Z]
    rows = near_ref.shape[1]
    for side, ref in enumerate((near_ref, far_ref)):
        for step in range(4):
            start = (4 * side + step) * rows
            held[start : start + rows] = ref[step if mirrored else place_ref[X] ^ step]
    for half, depths in enumerate(((1, 2), (3, 0))):
        for step in range(4):
            columns = []
            for depth in depths:
                column = z ^ depth ^ 3 if mirrored else z ^ depth
                start = pl.multiple_of(((y ^ step) * 4 + column) * 128, 128)
                columns.append(weight_ref[:, pl.ds(start, 128)])
            product = jnp.dot(
                held[...], jnp.concatenate(columns, axis=1), preferred_element_type=F32
            ).astype(BF)
            out_refs[4 * half + step][0] = product[:, :128]
            out_refs[4 * half + step][1] = product[:, 128:]


def merge(*refs):
    sources, targets = refs[:4], refs[4:]
    for index, target in enumerate(targets):
        total = sources[0][index].astype(F32)
        for source in sources[1:]:
            total += source[index].astype(F32)
        target[...] = total.astype(BF)


def updated(sources, state):
    total = sources[0][...].astype(F32)
    for source in sources[1:]:
        total += source[...].astype(F32)
    total = total.astype(BF).astype(F32)
    return (state.astype(F32) + total).astype(BF)


def merge_state(*refs):
    sources, state_ref, out_ref = refs[:4], refs[4], refs[5]
    out_ref[...] = updated(sources, state_ref[...])


def merge_last(place_ref, *refs):
    sources, state_ref, first_ref, out_ref = refs[:4], refs[4], refs[5], refs[6]
    result = updated(sources, state_ref[...]).astype(F32)
    result = jnp.where(place_ref[SECTION] == 0, first_ref[...].astype(F32), result).astype(BF)
    rows = out_ref.shape[1]
    for side in range(2):
        for step in range(4):
            owner = (place_ref[X] ^ step) * 2 + (place_ref[CORE] ^ side)
            start = (side * 4 + step) * rows
            out_ref[owner] = result[start : start + rows]


def lay_out(place_ref, *refs):
    y, z = place_ref[Y], place_ref[Z]
    out_ref = refs[-1]
    mirror = jnp.where(place_ref[SECTION] == 0, 0, 3)
    for step, ref in enumerate(refs[:-1]):
        for depth in range(4):
            index = (y ^ step) * 4 + (z ^ depth ^ mirror)
            for part in range(8):
                start = pl.multiple_of(index * 128 + part * 2048, 128)
                out_ref[:, pl.ds(start, 128)] = ref[depth, part]


def row_half(index, cache):
    halves = cache.reshape(2, GROUP, *cache.shape[1:])
    return lax.dynamic_index_in_dim(halves, index, 0, keepdims=False)


def spread(piece):
    return gathered(jnp.stack(gathered(piece, DEPTH)), "y")


def reduced(near, far):
    rows, wide = near.shape
    block = jax.ShapeDtypeStruct((rows // 4, wide), BF)
    sums = call(add_cores, [block] * 4, (near, moved(far, "c", 1)), name="add_cores")
    return [moved(s, "x", step) for step, s in enumerate(sums)]


def traded(blocks, axes):
    return lax.all_to_all(blocks, axes, split_axis=0, concat_axis=0, tiled=True)


def output(mirrored, near, place, out_weight, awaited=None):
    rows, wide = 8 * near.shape[1], near.shape[2]
    parts = call(
        functools.partial(emit, mirrored),
        [jax.ShapeDtypeStruct((2, rows, 128), BF)] * 8,
        (place, near, moved(near, "c", 1), out_weight),
        flops=2 * rows * wide * out_weight.shape[1],
        scratch=[pltpu.VMEM((rows, wide), BF)],
        name="emit",
    )
    parts = [moved(p, "y", step % 4) for step, p in enumerate(parts)]
    if awaited is not None:
        parts[0], awaited = lax.optimization_barrier((parts[0], awaited))
    share = jax.ShapeDtypeStruct((rows, 128), BF)
    one, two = call(merge, [share] * 2, parts[:4], name="merge")
    received = [moved(one, DEPTH, 1), moved(two, DEPTH, 2)]
    three, own = call(merge, [share] * 2, parts[4:], name="merge")
    return [own, *received, moved(three, DEPTH, 3)], awaited


def body(hidden, query_weight, out_weight, key_cache, value_cache, cache_lengths):
    place = jnp.stack([lax.axis_index(a) for a in ("y", DEPTH, "zl", "s", "x", "c")])
    place = place.astype(jnp.int32)
    rows, wide = hidden.shape
    part = wide // 8
    place = lax.optimization_barrier(place)
    query_weight, out_weight = query_weight[0], out_weight[0]
    key = jnp.swapaxes(key_cache[0], 1, 2)
    value = jnp.swapaxes(value_cache[0], 1, 2)
    half = lax.axis_index("zl").astype(jnp.int32)
    place, half = lax.optimization_barrier((place, half))
    near_half = jnp.stack([row_half(1 - half, key), row_half(1 - half, value)])
    near_half = moved(near_half, "zl", 1)
    sent = call(
        arrange,
        [jax.ShapeDtypeStruct((2, rows, part), BF)] * 4,
        (place, hidden),
        name="arrange",
    )
    blocks = [moved(b, "x", step) for step, b in enumerate(sent)]
    mine_key, mine_value = row_half(half, key), row_half(half, value)
    mine_key, mine_value, blocks[1] = lax.optimization_barrier((mine_key, mine_value, blocks[1]))
    other = call(pick, jax.ShapeDtypeStruct((4, rows, part), BF), blocks, name="pick")
    other = moved(other, "c", 1)
    partial = jax.ShapeDtypeStruct((4 * rows, query_weight.shape[1] + 128), BF)
    share = jax.ShapeDtypeStruct((8 * rows, 128), BF)
    held = pltpu.VMEM((8 * rows, part), BF)
    flops = 16 * rows * query_weight.shape[0] * query_weight.shape[1]
    near, far, state = call(
        project_rows,
        [partial, partial, share],
        (place, *blocks, other, query_weight),
        flops=flops,
        scratch=[held],
        name="project_rows",
    )
    far, near_half = lax.optimization_barrier((far, near_half))
    width = query_weight.shape[1]
    sums = call(
        add_cores_pair,
        jax.ShapeDtypeStruct((8, GROUP, width + 128), BF),
        (place, near, moved(far, "c", 1)),
        name="add_cores_pair",
    )
    attended = call(
        attend_pair,
        jax.ShapeDtypeStruct((8, GROUP, width), BF),
        (place, cache_lengths, traded(sums, ("x", "zl")), mine_key, mine_value, near_half),
        flops=8 * 8 * rows * 2048 * 256,
        name="attend_pair",
    )
    attended = traded(attended, ("x", "zl")).reshape(4, rows, width)
    mine_key, attended = lax.optimization_barrier((mine_key, attended))
    far_key = moved(mine_key, "zl", 1)
    parts, far_key = output(False, attended, place, out_weight, far_key)
    first = call(merge_state, share, (*parts, state), name="merge_state")

    arrived = moved(first, ("s", *DEPTH), 7)
    chunk = jnp.stack(gathered(arrived, DEPTH))
    chunk, mine_value = lax.optimization_barrier((chunk, mine_value))
    chunks = gathered(chunk, "y")
    far_value = moved(mine_value, "zl", 1)
    near, far = call(
        project_columns,
        [partial, partial],
        (place, *chunks, query_weight),
        flops=flops,
        scratch=[held],
        name="project_columns",
    )
    attended = call(
        attend,
        jax.ShapeDtypeStruct((rows, width), BF),
        (
            place,
            cache_lengths,
            *reduced(near, far),
            *(key, value, near_half, far_key, far_value),
        ),
        flops=8 * 8 * rows * 2048 * 256,
        name="attend",
    )
    near = call(pick, jax.ShapeDtypeStruct((4, rows, width), BF), gathered(attended, "x"), name="pick")
    parts, _ = output(True, near, place, out_weight)
    result = call(
        merge_last,
        jax.ShapeDtypeStruct((8, rows, 128), BF),
        (place, *parts, arrived, first),
        name="merge_last",
    )
    result = traded(result, DP)
    out = call(
        lay_out, jax.ShapeDtypeStruct((rows, wide), BF), (place, *spread(result)), name="lay_out"
    )
    return out[None]


def solution(mesh):
    fine = Mesh(mesh.devices.reshape(2, 4, 2, 4, 2, 2), ("s", "x", "c", "y", "zh", "zl"))
    in_specs = (
        P(DP, None),
        P("s", DP, TENSOR),
        P("s", TENSOR, DP),
        P("s", DP, None, TENSOR),
        P("s", DP, None, TENSOR),
        P(DP),
    )
    out_specs = P("s", DP, None)
    return jax.shard_map(body, mesh=fine, in_specs=in_specs, out_specs=out_specs, check_vma=False)
```
